512 devices in a mesh: frame: 64 (over z, x, core), segment: 8 (over y).
Axes of the slice: x: 4, y: 8, z: 8, core: 2. Of those that a mesh axis runs over, the one named last changes fastest.
Arguments:
- state: bfloat16 [8, 2048, 3072], P('segment', 'frame'), may hold values from -6 to 6
- modulation: float32 [8, 32, 7, 3072], P('segment'), may hold values from -3 to 3
- noise_level: int32 [8], replicated, may hold values from 0 to 31
- frame_mask: int32 [8, 8], replicated, may hold values from 0 to 1, as said below
- offset: int32 [1], replicated, may hold values from 1 to 7
Outputs:
- next_state: bfloat16 [8, 2048, 3072], P('segment', 'frame')
The draws below stay inside these ranges and needn't reach their ends.
Inputs may be any that keep to these rules, and one draw needn't show every extreme that they name: frame_mask[i, i] is 1 and frame_mask[i, j] is 0 for j > i.
All inputs are finite; a program needn't handle non-finite values.
Results may differ from the reference program's by a relative error of at most 0.017.
Values may be sent and summed in bfloat16 or wider, within the bound.
No kernel may reach another device: no remote copies, remote signals or barrier semaphores. Data moves between devices by JAX's collectives and lax.ppermute only.
A program may use at most 128 MiB of HBM per device.

```python
import math
import jax
import jax.numpy as jnp
from jax import lax

D = 3072
HEADS = 24
HEAD = 128
LEVELS = 32
FRAME_TOK = 256
FRAMES = 8
TOKENS = 2048
N_SEGMENT = 8


def draw_frame_mask(key, part):
    frames_all = TOKENS // FRAME_TOK
    picks = jax.random.randint(jax.random.fold_in(key, 17), (frames_all, frames_all), 0, 4)
    row_ids = jnp.arange(frames_all, dtype=jnp.int32)[:, None]
    col_ids = jnp.arange(frames_all, dtype=jnp.int32)[None, :]
    earlier = jnp.where(picks > 0, 1, 0)
    return jnp.where(row_ids > col_ids, earlier, jnp.where(row_ids == col_ids, 1, 0)).astype(jnp.int32)


def draw_state(key, part):
    frames_all = TOKENS // FRAME_TOK
    background_share = 0.3
    carry_rate = 0.4 ** (1.0 / frames_all)
    fresh = jax.random.normal(jax.random.fold_in(key, 5), (N_SEGMENT, frames_all, FRAME_TOK * D), jnp.float32)
    frame_ids = jnp.arange(frames_all, dtype=jnp.int32)
    lag = frame_ids[:, None] - frame_ids[None, :]
    lag_float = jnp.maximum(lag, 0).astype(jnp.float32)
    entry_scale = jnp.where(frame_ids[None, :] == 0, 1.0, math.sqrt(1.0 - carry_rate * carry_rate))
    mixing = jnp.where(lag >= 0, jnp.power(jnp.float32(carry_rate), lag_float) * entry_scale, 0.0).astype(jnp.float32)
    carried = jnp.einsum('fg,sgc->sfc', mixing, fresh, precision=lax.Precision.HIGHEST)
    carried = carried.reshape(N_SEGMENT, frames_all, FRAME_TOK, D)
    backdrop = jax.random.normal(jax.random.fold_in(key, 9), (N_SEGMENT, D), jnp.float32)
    backdrop = backdrop / jnp.sqrt(jnp.mean(backdrop * backdrop, axis=-1, keepdims=True))
    framed = math.sqrt(background_share) * backdrop[:, None, None, :] + math.sqrt(1.0 - background_share) * carried
    noise_field = framed.reshape(N_SEGMENT, TOKENS, D)
    return jnp.clip(noise_field, -6.0, 6.0).astype(jnp.bfloat16)


def plant(values, own_key, low, high):
    shape = values.shape
    spot = [jax.random.randint(jax.random.fold_in(own_key, axis), (), 0, shape[axis]) for axis in range(len(shape))]
    values = values.at[tuple(spot)].set(low)
    longest = shape.index(max(shape))
    spot[longest] = (spot[longest] + 1) % shape[longest]
    return values.at[tuple(spot)].set(high)


def steps_of(stream_key, extent, split, least, top_value):
    loudness, own = 1.0, jax.random.fold_in(stream_key, 6)
    for dim, parts in split:
        heights = jnp.exp(jax.random.uniform(jax.random.fold_in(own, dim), (parts,), jnp.float32, least / len(split), top_value / len(split)))
        loudness = loudness * jnp.repeat(heights, extent[dim] // parts).reshape([-1 if axis == dim else 1 for axis in range(len(extent))])
    return loudness


def centred(stream_key, dims, deviation, most, cuts=(), kind=jnp.bfloat16):
    values = deviation * jax.random.normal(stream_key, dims, jnp.float32)
    if cuts:
        values = values * steps_of(stream_key, dims, cuts, -0.22, 0.18)
    return jnp.clip(values, -most, most).astype(kind)


def setup_inputs(seed: int = 0) -> dict:
    keys = jax.random.split(jax.random.key(seed), 6)
    return {
        "state": draw_state(jax.random.fold_in(keys[5], 71), 0),
        "modulation": centred(keys[1], (N_SEGMENT, LEVELS, 7, D), 0.5, 3.0, ((0, 8),), jnp.float32),
        "noise_level": plant(jax.random.randint(keys[2], (FRAMES,), 0, LEVELS), jax.random.fold_in(keys[2], 1), 0, LEVELS - 1).astype(jnp.int32),
        "frame_mask": draw_frame_mask(jax.random.fold_in(keys[5], 71), 0),
        "offset": jax.random.randint(keys[4], (1,), 1, FRAMES).astype(jnp.int32),
    }


epsilon = 1e-06

def normalize(values):
    widened = values.astype(jnp.float32)
    square_mean = lax.optimization_barrier(jnp.mean(widened * widened, axis=-1, keepdims=True))
    return (widened * lax.rsqrt(square_mean + epsilon)).astype(jnp.bfloat16)

def modulate(normed, modifiers, column):
    scaled = normed.astype(jnp.float32) * (1.0 + modifiers[:, column]) + modifiers[:, column + 1]
    return scaled.astype(jnp.bfloat16)

def section(hidden, level_table, noise_level, frame_mask):
    tokens_all = hidden.shape[0]
    row_frames = jnp.arange(tokens_all, dtype=jnp.int32) // FRAME_TOK
    modifiers = level_table[noise_level[row_frames]]
    normed = normalize(hidden)
    queries = modulate(normed, modifiers, 0)
    keys_all = modulate(normed, modifiers, 2)
    values_all = modulate(normed, modifiers, 4)
    allowed = frame_mask[row_frames][:, row_frames] == 1
    scale_factor = 1.0 / math.sqrt(HEAD)

    def split_heads(rows):
        return jnp.transpose(rows.reshape(tokens_all, HEADS, HEAD), (1, 0, 2))

    def per_head(stacked):
        query_head, key_head, value_head = stacked
        scores = jnp.dot(query_head, key_head.T, preferred_element_type=jnp.float32) * scale_factor
        scores = jnp.where(allowed, scores, jnp.float32(-1e+30))
        row_max = lax.optimization_barrier(jnp.max(scores, axis=-1, keepdims=True))
        weights = jnp.where(allowed, jnp.exp(scores - row_max), jnp.float32(0.0)).astype(jnp.bfloat16)
        summed = jnp.dot(weights, value_head, preferred_element_type=jnp.float32)
        denominator = lax.optimization_barrier(jnp.sum(weights.astype(jnp.float32), axis=-1, keepdims=True))
        return (summed / denominator).astype(jnp.bfloat16)
    heads_out = lax.map(per_head, (split_heads(queries), split_heads(keys_all), split_heads(values_all)))
    attention = jnp.transpose(heads_out, (1, 0, 2)).reshape(tokens_all, HEADS * HEAD)
    updated = hidden.astype(jnp.float32) + modifiers[:, 6] * attention.astype(jnp.float32)
    return updated.astype(jnp.bfloat16)

def reference(state, modulation, noise_level, frame_mask, offset):
    outputs = [section(state[segment_num], modulation[segment_num], noise_level, frame_mask) for segment_num in range(N_SEGMENT)]
    wrapped = jnp.roll(outputs[-1], -offset[0] * FRAME_TOK, axis=0)
    return jnp.stack([wrapped] + outputs[:-1])
```

```python
import math

import jax
import jax.numpy as jnp
from jax import lax
from jax.experimental import pallas as pl
from jax.experimental.pallas import tpu as pltpu
from jax.sharding import PartitionSpec as P

HEAD = 128
HEADS = 24
WIDTH = HEAD * HEADS
FRAMES = 8
ROWS = 32
SLOT = ROWS + 8
CHIPS = 32
PER_FRAME = CHIPS // FRAMES
HALF = PER_FRAME * ROWS
COLUMNS = 7

epsilon = 1e-06
negative = -1e30

VMEM = pl.BlockSpec(memory_space=pltpu.VMEM)
SMEM = pl.BlockSpec(memory_space=pltpu.SMEM)
ANY = pl.BlockSpec(memory_space=pl.ANY)


def pack_kernel(state, packed):
    wide = state[...].astype(jnp.float32)
    factor = lax.rsqrt(jnp.sum(wide * wide, axis=-1, keepdims=True) * (1.0 / WIDTH) + epsilon)
    high = factor.astype(jnp.bfloat16).astype(jnp.float32)
    middle = (factor - high).astype(jnp.bfloat16).astype(jnp.float32)
    low = factor - high - middle
    lane = lax.broadcasted_iota(jnp.int32, (8, HEAD), 1)
    factors = jnp.zeros((8, HEAD), jnp.float32)
    for group in range(ROWS // 8):
        for at, piece in enumerate((high, middle, low)):
            rows = jnp.broadcast_to(piece[8 * group : 8 * group + 8], (8, HEAD))
            factors = jnp.where(lane == 32 * group + at, rows, factors)
    for two in range(HEADS // 2):
        a, b = 2 * two, 2 * two + 1
        packed[2 * SLOT * two : 2 * SLOT * (two + 1), :] = jnp.concatenate(
            [
                wide[:, HEAD * a : HEAD * (a + 1)],
                factors,
                wide[:, HEAD * b : HEAD * (b + 1)],
                factors,
            ],
            axis=0,
        ).astype(jnp.bfloat16)
    packed[HEADS * SLOT :, :] = jnp.zeros(((CHIPS - HEADS) * SLOT, HEAD), jnp.bfloat16)


def pick_kernel(levels, table, mods, column, sem):
    head = jnp.minimum(lax.axis_index("frame") // 2, HEADS - 1)
    copy = pltpu.make_async_copy(
        table.at[:, :, pl.ds(pl.multiple_of(head * HEAD, HEAD), HEAD)], column, sem
    )
    copy.start()
    copy.wait()
    for frame in range(FRAMES):
        level = levels[frame]
        for c in range(COLUMNS):
            mods[8 * frame + c : 8 * frame + c + 1, :] = column[c, pl.ds(level, 1), :]


def unpacked(chunk):
    wide = chunk.astype(jnp.float32)
    state, factor = [], []
    for slot in range(PER_FRAME):
        at = SLOT * slot
        state.append(wide[at : at + ROWS])
        pieces = wide[at + ROWS : at + SLOT]
        for group in range(ROWS // 8):
            lane = 32 * group
            whole = (
                pieces[:, lane : lane + 1] + pieces[:, lane + 1 : lane + 2]
            ) + pieces[:, lane + 2 : lane + 3]
            factor.append(jnp.broadcast_to(whole, (8, HEAD)))
    state = jnp.concatenate(state, axis=0)
    normed = (state * jnp.concatenate(factor, axis=0)).astype(jnp.bfloat16)
    return state, normed.astype(jnp.float32)


def attend_kernel(offset, mask, mods, slots, out, keys, values, queries, kept, scores):
    core = lax.rem(lax.axis_index("frame"), 2)
    last = lax.axis_index("segment") == lax.axis_size("segment") - 1
    shift = jnp.where(last, offset[0], 0)
    ones = jnp.ones((16, 2 * HALF), jnp.bfloat16)

    def rows_of(frame, c):
        return mods[8 * frame + c : 8 * frame + c + 1, :]

    for frame in range(FRAMES):
        for part in range(2):
            at = CHIPS * SLOT * part + PER_FRAME * SLOT * frame
            _unused, normed = unpacked(slots[at : at + PER_FRAME * SLOT, :])
            key = normed * (1.0 + rows_of(frame, 2)) + rows_of(frame, 3)
            value = normed * (1.0 + rows_of(frame, 4)) + rows_of(frame, 5)
            row = 2 * HALF * frame + HALF * part
            keys[row : row + HALF, :] = key.astype(jnp.bfloat16)
            values[frame, :HEAD, HALF * part : HALF * (part + 1)] = value.T.astype(jnp.bfloat16)
        values[frame, HEAD:, :] = ones
        at = pl.multiple_of(CHIPS * SLOT * core + PER_FRAME * SLOT * frame, 16)
        state, normed = unpacked(slots[pl.ds(at, PER_FRAME * SLOT), :])
        query = normed * (1.0 + rows_of(frame, 0)) + rows_of(frame, 1)
        side = HALF * (frame % 2)
        queries[frame // 2, :, side : side + HALF] = query.T.astype(jnp.bfloat16)
        kept[HALF * frame : HALF * (frame + 1), :] = state

    side = lax.broadcasted_iota(jnp.int32, (1, 2 * HALF), 1) < HALF
    rate = math.log2(math.e) / math.sqrt(HEAD)
    for two in range(FRAMES // 2):
        first, second = 2 * two, 2 * two + 1
        query = queries[two]
        top = jnp.full((8, 2 * HALF), negative, jnp.float32)
        for frame in range(second + 1):
            barred = jnp.where(
                side,
                jnp.where(mask[first, frame] == 1, 0.0, negative),
                jnp.where(mask[second, frame] == 1, 0.0, negative),
            )
            here = slice(2 * HALF * frame, 2 * HALF * (frame + 1))
            got = jnp.dot(keys[here, :], query, preferred_element_type=jnp.float32) + barred
            scores[here, :] = got
            top = jnp.maximum(top, jnp.max(got.reshape(2 * HALF // 8, 8, 2 * HALF), axis=0))
        top = jnp.max(top, axis=0, keepdims=True)
        total = jnp.zeros((HEAD + 16, 2 * HALF), jnp.float32)
        for frame in range(second + 1):
            here = slice(2 * HALF * frame, 2 * HALF * (frame + 1))
            weights = jnp.exp2((scores[here, :] - top) * rate).astype(jnp.bfloat16)
            total = total + jnp.dot(values[frame], weights, preferred_element_type=jnp.float32)
        attention = total[:HEAD] * (1.0 / total[HEAD : HEAD + 1])
        attention = attention.astype(jnp.bfloat16).astype(jnp.float32).T
        for frame in (first, second):
            rows = attention[HALF * (frame - first) : HALF * (frame - first + 1)]
            updated = kept[HALF * frame : HALF * (frame + 1), :] + rows_of(frame, 6) * rows
            to = pl.multiple_of(HALF * lax.rem(frame + FRAMES - shift, FRAMES), HALF)
            out[pl.ds(to, HALF), :] = updated.astype(jnp.bfloat16)


def body(state, modulation, noise_level, frame_mask, offset):
    segments = lax.axis_size("segment")
    table = jnp.transpose(modulation[0], (1, 0, 2))
    same_core = [[2 * chip + core for chip in range(CHIPS)] for core in range(2)]
    same_chip = [[2 * chip, 2 * chip + 1] for chip in range(CHIPS)]

    packed = pl.pallas_call(
        pack_kernel,
        out_shape=jax.ShapeDtypeStruct((CHIPS * SLOT, HEAD), jnp.bfloat16),
        in_specs=[VMEM],
        out_specs=VMEM,
        compiler_params=pltpu.CompilerParams(vmem_limit_bytes=8 * 2**20),
        name="pack",
    )(state[0])
    mods = pl.pallas_call(
        pick_kernel,
        out_shape=jax.ShapeDtypeStruct((8 * FRAMES, HEAD), jnp.float32),
        in_specs=[SMEM, ANY],
        out_specs=VMEM,
        scratch_shapes=[
            pltpu.VMEM((COLUMNS, modulation.shape[1], HEAD), jnp.float32),
            pltpu.SemaphoreType.DMA,
        ],
        compiler_params=pltpu.CompilerParams(vmem_limit_bytes=8 * 2**20),
        name="pick",
    )(noise_level, table)
    heads = lax.all_to_all(packed, "frame", 0, 0, axis_index_groups=same_core, tiled=True)
    slots = lax.all_gather(heads, "frame", axis=0, tiled=True, axis_index_groups=same_chip)
    done = pl.pallas_call(
        attend_kernel,
        out_shape=jax.ShapeDtypeStruct((CHIPS * ROWS, HEAD), jnp.bfloat16),
        in_specs=[SMEM, SMEM, VMEM, VMEM],
        out_specs=VMEM,
        scratch_shapes=[
            pltpu.VMEM((FRAMES * 2 * HALF, HEAD), jnp.bfloat16),
            pltpu.VMEM((FRAMES, HEAD + 16, 2 * HALF), jnp.bfloat16),
            pltpu.VMEM((FRAMES // 2, HEAD, 2 * HALF), jnp.bfloat16),
            pltpu.VMEM((FRAMES * HALF, HEAD), jnp.float32),
            pltpu.VMEM((FRAMES * 2 * HALF, 2 * HALF), jnp.float32),
        ],
        compiler_params=pltpu.CompilerParams(vmem_limit_bytes=24 * 2**20),
        name="attend",
    )(offset, frame_mask, mods, slots)
    back = lax.all_to_all(done, "frame", 0, 0, axis_index_groups=same_core, tiled=True)
    rows = jnp.transpose(back[: HEADS * ROWS].reshape(HEADS, ROWS, HEAD), (1, 0, 2))
    passed = lax.ppermute(
        rows.reshape(ROWS, WIDTH), "segment", [(i, (i + 1) % segments) for i in range(segments)]
    )
    return passed[None]


def solution(mesh):
    return jax.shard_map(
        body,
        mesh=mesh,
        in_specs=(P("segment", "frame", None), P("segment", None, None, None), P(), P(), P()),
        out_specs=P("segment", "frame", None),
        check_vma=False,
    )
```

```python
import math

import jax
import jax.numpy as jnp
from jax import lax
from jax.experimental import pallas as pl
from jax.experimental.pallas import tpu as pltpu
from jax.sharding import PartitionSpec as P

HEAD = 128
HEADS = 24
WIDTH = HEAD * HEADS
FRAMES = 8
ROWS = 32
SLOT = ROWS + 8
CHIPS = 32
PER_FRAME = CHIPS // FRAMES
HALF = PER_FRAME * ROWS
COLUMNS = 7

epsilon = 1e-06
negative = -1e30

VMEM = pl.BlockSpec(memory_space=pltpu.VMEM)
SMEM = pl.BlockSpec(memory_space=pltpu.SMEM)
ANY = pl.BlockSpec(memory_space=pl.ANY)


def pack_kernel(state, packed):
    wide = state[...].astype(jnp.float32)
    factor = lax.rsqrt(jnp.sum(wide * wide, axis=-1, keepdims=True) * (1.0 / WIDTH) + epsilon)
    high = factor.astype(jnp.bfloat16).astype(jnp.float32)
    middle = (factor - high).astype(jnp.bfloat16).astype(jnp.float32)
    low = factor - high - middle
    lane = lax.broadcasted_iota(jnp.int32, (8, HEAD), 1)
    factors = jnp.zeros((8, HEAD), jnp.float32)
    for group in range(ROWS // 8):
        for at, piece in enumerate((high, middle, low)):
            rows = jnp.broadcast_to(piece[8 * group : 8 * group + 8], (8, HEAD))
            factors = jnp.where(lane == 32 * group + at, rows, factors)
    for two in range(CHIPS // 2):
        pieces = []
        for slot in (2 * two, 2 * two + 1):
            chip = PER_FRAME * (FRAMES - 1 - slot // PER_FRAME) + slot % PER_FRAME
            head = min(chip, HEADS - 1)
            pieces += [wide[:, HEAD * head : HEAD * (head + 1)], factors]
        both = jnp.concatenate(pieces, axis=0)
        packed[2 * SLOT * two : 2 * SLOT * (two + 1), :] = both.astype(jnp.bfloat16)


def pick_kernel(levels, table, mods, column, sem):
    head = jnp.minimum(lax.axis_index("frame") // 2, HEADS - 1)
    copy = pltpu.make_async_copy(
        table.at[:, :, pl.ds(pl.multiple_of(head * HEAD, HEAD), HEAD)], column, sem
    )
    copy.start()
    copy.wait()
    for frame in range(FRAMES):
        level = levels[frame]
        for c in range(COLUMNS):
            mods[8 * frame + c : 8 * frame + c + 1, :] = column[c, pl.ds(level, 1), :]


def attend_kernel(
    offset, mask, mods, slots, out, factors, normed, keys, values, queries, scores
):
    core = lax.rem(lax.axis_index("frame"), 2)
    last = lax.axis_index("segment") == lax.axis_size("segment") - 1
    shift = jnp.where(last, offset[0], 0)
    chunk = PER_FRAME * SLOT

    def rows_of(frame, c):
        return mods[8 * frame + c : 8 * frame + c + 1, :]

    quarter = lax.broadcasted_iota(jnp.int32, (HEAD, HEAD), 0) >> 5
    spread = jnp.concatenate(
        [jnp.where(quarter == group, 1.0, 0.0) for group in range(ROWS // 8)], axis=1
    ).astype(jnp.bfloat16)
    for part in range(2):
        pieces = []
        for frame in range(FRAMES):
            at = CHIPS * SLOT * part + chunk * (FRAMES - 1 - frame)
            wide = slots[at : at + chunk, :].astype(jnp.float32)
            for slot in range(PER_FRAME):
                pieces.append(wide[SLOT * slot + ROWS : SLOT * (slot + 1)])
        pieces = jnp.concatenate(pieces, axis=0).astype(jnp.bfloat16)
        factors[part] = jnp.dot(pieces, spread, preferred_element_type=jnp.float32)

    def state_of(wide):
        return jnp.concatenate(
            [wide[SLOT * slot : SLOT * slot + ROWS] for slot in range(PER_FRAME)], axis=0
        )

    def prepare(frame):
        for part in range(2):
            at = CHIPS * SLOT * part + chunk * (FRAMES - 1 - frame)
            state = state_of(slots[at : at + chunk, :].astype(jnp.float32))
            factor = jnp.concatenate(
                [
                    factors[
                        part,
                        8 * (PER_FRAME * frame + slot) : 8 * (PER_FRAME * frame + slot + 1),
                        HEAD * group : HEAD * (group + 1),
                    ]
                    for slot in range(PER_FRAME)
                    for group in range(ROWS // 8)
                ],
                axis=0,
            )
            even = (state * factor).astype(jnp.bfloat16).astype(jnp.float32)
            normed[part, HALF * frame : HALF * (frame + 1), :] = even
            key = even * (1.0 + rows_of(frame, 2)) + rows_of(frame, 3)
            value = even * (1.0 + rows_of(frame, 4)) + rows_of(frame, 5)
            row = 2 * HALF * frame + HALF * part
            keys[row : row + HALF, :] = key.astype(jnp.bfloat16)
            values[frame, :HEAD, HALF * part : HALF * (part + 1)] = value.astype(jnp.bfloat16).T
        values[frame, HEAD:, :] = jnp.ones((16, 2 * HALF), jnp.bfloat16)
        even = normed[core, HALF * frame : HALF * (frame + 1), :]
        query = even * (1.0 + rows_of(frame, 0)) + rows_of(frame, 1)
        half = HALF * (frame % 2)
        queries[frame // 2, :, half : half + HALF] = query.astype(jnp.bfloat16).T

    side = lax.broadcasted_iota(jnp.int32, (1, 2 * HALF), 1) < HALF
    rate = math.log2(math.e) / math.sqrt(HEAD)
    wide = 2 * HALF
    scored, weighed = {}, {}

    def score(two, frame):
        barred = jnp.where(
            side,
            jnp.where(mask[2 * two, frame] == 1, 0.0, negative),
            jnp.where(mask[2 * two + 1, frame] == 1, 0.0, negative),
        )
        got = jnp.dot(
            keys[wide * frame : wide * (frame + 1), :],
            queries[two],
            preferred_element_type=jnp.float32,
        )
        scores[two * (two + 1) + frame] = got
        high = jnp.max(got.reshape(wide // 8, 8, wide), axis=0) + barred
        top, bars = scored.get(two, (None, []))
        scored[two] = (high if top is None else jnp.maximum(top, high), [*bars, barred])

    def weigh(two, frame):
        top, bars = scored[two]
        if frame == 0:
            top = jnp.max(top, axis=0, keepdims=True)
            scored[two] = (top, bars)
        less = top - bars[frame]
        weights = jnp.exp2((scores[two * (two + 1) + frame] - less) * rate)
        part = jnp.dot(
            values[frame], weights.astype(jnp.bfloat16), preferred_element_type=jnp.float32
        )
        weighed[two] = part if frame == 0 else weighed[two] + part

    def finish(two):
        total = weighed.pop(two)
        attention = total[:HEAD] * (1.0 / total[HEAD : HEAD + 1])
        attention = attention.astype(jnp.bfloat16).astype(jnp.float32).T
        for side_of, frame in enumerate((2 * two, 2 * two + 1)):
            at = pl.multiple_of(CHIPS * SLOT * core + chunk * (FRAMES - 1 - frame), 16)
            state = state_of(slots[pl.ds(at, chunk), :].astype(jnp.float32))
            rows = attention[HALF * side_of : HALF * (side_of + 1)]
            to = FRAMES - 1 - lax.rem(frame + FRAMES - shift, FRAMES)
            to = pl.multiple_of(HALF * to, HALF)
            out[pl.ds(to, HALF), :] = (state + rows_of(frame, 6) * rows).astype(jnp.bfloat16)

    for frame in range(FRAMES):
        prepare(frame)
        if frame >= 2:
            two = frame // 2 - 1
            for other in range(two + 1):
                score(two, other + (frame % 2) * (two + 1))
    last_pair = FRAMES // 2 - 1
    steps = [(score, last_pair, other) for other in range(FRAMES)]
    for two in reversed(range(last_pair)):
        for frame in range(2 * two + 2):
            if steps:
                step, pair, other = steps.pop(0)
                step(pair, other)
            weigh(two, frame)
        finish(two)
    for frame in range(FRAMES):
        weigh(last_pair, frame)
    finish(last_pair)


def body(state, modulation, noise_level, frame_mask, offset):
    segments = lax.axis_size("segment")
    table = jnp.transpose(modulation[0], (1, 0, 2))
    same_core = [
        [2 * (PER_FRAME * frame + x) + core for frame in reversed(range(FRAMES)) for x in range(PER_FRAME)]
        for core in range(2)
    ]
    same_chip = [[2 * chip, 2 * chip + 1] for chip in range(CHIPS)]

    packed = pl.pallas_call(
        pack_kernel,
        out_shape=jax.ShapeDtypeStruct((CHIPS * SLOT, HEAD), jnp.bfloat16),
        in_specs=[VMEM],
        out_specs=VMEM,
        compiler_params=pltpu.CompilerParams(vmem_limit_bytes=8 * 2**20),
        name="pack",
    )(state[0])
    mods = pl.pallas_call(
        pick_kernel,
        out_shape=jax.ShapeDtypeStruct((8 * FRAMES, HEAD), jnp.float32),
        in_specs=[SMEM, ANY],
        out_specs=VMEM,
        scratch_shapes=[
            pltpu.VMEM((COLUMNS, modulation.shape[1], HEAD), jnp.float32),
            pltpu.SemaphoreType.DMA,
        ],
        compiler_params=pltpu.CompilerParams(vmem_limit_bytes=8 * 2**20),
        name="pick",
    )(noise_level, table)
    heads = lax.all_to_all(packed, "frame", 0, 0, axis_index_groups=same_core, tiled=True)
    slots = lax.all_gather(heads, "frame", axis=0, tiled=True, axis_index_groups=same_chip)
    done = pl.pallas_call(
        attend_kernel,
        out_shape=jax.ShapeDtypeStruct((CHIPS * ROWS, HEAD), jnp.bfloat16),
        in_specs=[SMEM, SMEM, VMEM, VMEM],
        out_specs=VMEM,
        scratch_shapes=[
            pltpu.VMEM((2, 8 * CHIPS, ROWS // 8 * HEAD), jnp.float32),
            pltpu.VMEM((2, FRAMES * HALF, HEAD), jnp.float32),
            pltpu.VMEM((FRAMES * 2 * HALF, HEAD), jnp.bfloat16),
            pltpu.VMEM((FRAMES, HEAD + 16, 2 * HALF), jnp.bfloat16),
            pltpu.VMEM((FRAMES // 2, HEAD, 2 * HALF), jnp.bfloat16),
            pltpu.VMEM((20, 2 * HALF, 2 * HALF), jnp.float32),
        ],
        compiler_params=pltpu.CompilerParams(vmem_limit_bytes=24 * 2**20),
        name="attend",
    )(offset, frame_mask, mods, slots)
    back = lax.all_to_all(done, "frame", 0, 0, axis_index_groups=same_core, tiled=True)
    back = back.reshape(FRAMES, PER_FRAME, ROWS, HEAD)[FRAMES - HEADS // PER_FRAME :][::-1]
    rows = jnp.transpose(back.reshape(HEADS, ROWS, HEAD), (1, 0, 2)).reshape(ROWS, WIDTH)
    passed = lax.ppermute(
        rows, "segment", [(i, (i + 1) % segments) for i in range(segments)]
    )
    return passed[None]


def solution(mesh):
    return jax.shard_map(
        body,
        mesh=mesh,
        in_specs=(P("segment", "frame", None), P("segment", None, None, None), P(), P(), P()),
        out_specs=P("segment", "frame", None),
        check_vma=False,
    )
```

```python
import math

import jax
import jax.numpy as jnp
from jax import lax
from jax.experimental import pallas as pl
from jax.experimental.pallas import tpu as pltpu
from jax.sharding import PartitionSpec as P

HEAD = 128
HEADS = 24
WIDTH = HEAD * HEADS
FRAMES = 8
ROWS = 32
SLOT = ROWS + 8
CHIPS = 32
PER_FRAME = CHIPS // FRAMES
HALF = PER_FRAME * ROWS
COLUMNS = 7

epsilon = 1e-06
negative = -1e30

VMEM = pl.BlockSpec(memory_space=pltpu.VMEM)
SMEM = pl.BlockSpec(memory_space=pltpu.SMEM)
ANY = pl.BlockSpec(memory_space=pl.ANY)


def pack_kernel(state, packed):
    wide = state[...].astype(jnp.float32)
    factor = lax.rsqrt(jnp.sum(wide * wide, axis=-1, keepdims=True) * (1.0 / WIDTH) + epsilon)
    high = factor.astype(jnp.bfloat16).astype(jnp.float32)
    middle = (factor - high).astype(jnp.bfloat16).astype(jnp.float32)
    low = factor - high - middle
    lane = lax.broadcasted_iota(jnp.int32, (8, HEAD), 1)
    factors = jnp.zeros((8, HEAD), jnp.float32)
    for group in range(ROWS // 8):
        for at, piece in enumerate((high, middle, low)):
            rows = jnp.broadcast_to(piece[8 * group : 8 * group + 8], (8, HEAD))
            factors = jnp.where(lane == 32 * group + at, rows, factors)
    for two in range(CHIPS // 2):
        pieces = []
        for slot in (2 * two, 2 * two + 1):
            head = min(CHIPS - 1 - slot, HEADS - 1)
            pieces += [wide[:, HEAD * head : HEAD * (head + 1)], factors]
        both = jnp.concatenate(pieces, axis=0)
        packed[2 * SLOT * two : 2 * SLOT * (two + 1), :] = both.astype(jnp.bfloat16)


def pick_kernel(levels, table, mods, column, sem):
    head = jnp.minimum(lax.axis_index("frame") // 2, HEADS - 1)
    copy = pltpu.make_async_copy(
        table.at[:, :, pl.ds(pl.multiple_of(head * HEAD, HEAD), HEAD)], column, sem
    )
    copy.start()
    copy.wait()
    for frame in range(FRAMES):
        level = levels[frame]
        for c in range(COLUMNS):
            mods[8 * frame + c : 8 * frame + c + 1, :] = column[c, pl.ds(level, 1), :]


def attend_kernel(
    offset, mask, mods, slots, out, factors, normed, keys, values, queries, scores
):
    core = lax.rem(lax.axis_index("frame"), 2)
    last = lax.axis_index("segment") == lax.axis_size("segment") - 1
    shift = jnp.where(last, offset[0], 0)
    chunk = PER_FRAME * SLOT

    def rows_of(frame, c):
        return mods[8 * frame + c : 8 * frame + c + 1, :]

    quarter = lax.broadcasted_iota(jnp.int32, (HEAD, HEAD), 0) >> 5
    spread = jnp.concatenate(
        [jnp.where(quarter == group, 1.0, 0.0) for group in range(ROWS // 8)], axis=1
    ).astype(jnp.bfloat16)
    for part in range(2):
        pieces = []
        for frame in range(FRAMES):
            at = CHIPS * SLOT * part + chunk * (FRAMES - 1 - frame)
            wide = slots[at : at + chunk, :].astype(jnp.float32)
            for slot in range(PER_FRAME):
                pieces.append(wide[SLOT * slot + ROWS : SLOT * (slot + 1)])
        pieces = jnp.concatenate(pieces, axis=0).astype(jnp.bfloat16)
        factors[part] = jnp.dot(pieces, spread, preferred_element_type=jnp.float32)

    def state_of(wide):
        return jnp.concatenate(
            [wide[SLOT * slot : SLOT * slot + ROWS] for slot in range(PER_FRAME)], axis=0
        )

    def prepare(frame):
        for part in range(2):
            at = CHIPS * SLOT * part + chunk * (FRAMES - 1 - frame)
            state = state_of(slots[at : at + chunk, :].astype(jnp.float32))
            factor = jnp.concatenate(
                [
                    factors[
                        part,
                        8 * (PER_FRAME * frame + slot) : 8 * (PER_FRAME * frame + slot + 1),
                        HEAD * group : HEAD * (group + 1),
                    ]
                    for slot in range(PER_FRAME)
                    for group in range(ROWS // 8)
                ],
                axis=0,
            )
            even = (state * factor).astype(jnp.bfloat16).astype(jnp.float32)
            normed[part, HALF * frame : HALF * (frame + 1), :] = even
            key = even * (1.0 + rows_of(frame, 2)) + rows_of(frame, 3)
            value = even * (1.0 + rows_of(frame, 4)) + rows_of(frame, 5)
            row = 2 * HALF * frame + HALF * part
            keys[row : row + HALF, :] = key.astype(jnp.bfloat16)
            values[frame, :HEAD, HALF * part : HALF * (part + 1)] = value.astype(jnp.bfloat16).T
        values[frame, HEAD:, :] = jnp.ones((16, 2 * HALF), jnp.bfloat16)
        even = normed[core, HALF * frame : HALF * (frame + 1), :]
        query = even * (1.0 + rows_of(frame, 0)) + rows_of(frame, 1)
        half = HALF * (frame % 2)
        queries[frame // 2, :, half : half + HALF] = query.astype(jnp.bfloat16).T

    side = lax.broadcasted_iota(jnp.int32, (1, 2 * HALF), 1) < HALF
    rate = math.log2(math.e) / math.sqrt(HEAD)
    wide = 2 * HALF
    scored, weighed = {}, {}

    def score(two, frame):
        barred = jnp.where(
            side,
            jnp.where(mask[2 * two, frame] == 1, 0.0, negative),
            jnp.where(mask[2 * two + 1, frame] == 1, 0.0, negative),
        )
        got = jnp.dot(
            keys[wide * frame : wide * (frame + 1), :],
            queries[two],
            preferred_element_type=jnp.float32,
        )
        scores[two * (two + 1) + frame] = got
        high = jnp.max(got.reshape(wide // 8, 8, wide), axis=0) + barred
        top, bars = scored.get(two, (None, []))
        scored[two] = (high if top is None else jnp.maximum(top, high), [*bars, barred])

    def weigh(two, frame):
        top, bars = scored[two]
        if frame == 0:
            top = jnp.max(top, axis=0, keepdims=True)
            scored[two] = (top, bars)
        less = top - bars[frame]
        weights = jnp.exp2((scores[two * (two + 1) + frame] - less) * rate)
        part = jnp.dot(
            values[frame], weights.astype(jnp.bfloat16), preferred_element_type=jnp.float32
        )
        weighed[two] = part if frame == 0 else weighed[two] + part

    def finish(two):
        total = weighed.pop(two)
        attention = total[:HEAD] * (1.0 / total[HEAD : HEAD + 1])
        attention = attention.astype(jnp.bfloat16).astype(jnp.float32).T
        for side_of, frame in enumerate((2 * two, 2 * two + 1)):
            at = pl.multiple_of(CHIPS * SLOT * core + chunk * (FRAMES - 1 - frame), 16)
            state = state_of(slots[pl.ds(at, chunk), :].astype(jnp.float32))
            rows = attention[HALF * side_of : HALF * (side_of + 1)]
            to = FRAMES - 1 - lax.rem(frame + FRAMES - shift, FRAMES)
            to = pl.multiple_of(HALF * to, HALF)
            out[pl.ds(to, HALF), :] = (state + rows_of(frame, 6) * rows).astype(jnp.bfloat16)

    for frame in range(FRAMES):
        prepare(frame)
        if frame >= 2:
            two = frame // 2 - 1
            for other in range(two + 1):
                score(two, other + (frame % 2) * (two + 1))
    last_pair = FRAMES // 2 - 1
    steps = [(score, last_pair, other) for other in range(FRAMES)]
    for two in reversed(range(last_pair)):
        for frame in range(2 * two + 2):
            if steps:
                step, pair, other = steps.pop(0)
                step(pair, other)
            weigh(two, frame)
        finish(two)
    for frame in range(FRAMES):
        weigh(last_pair, frame)
    finish(last_pair)


def body(state, modulation, noise_level, frame_mask, offset):
    segments = lax.axis_size("segment")
    table = jnp.transpose(modulation[0], (1, 0, 2))
    same_core = [[2 * chip + core for chip in reversed(range(CHIPS))] for core in range(2)]
    same_chip = [[2 * chip, 2 * chip + 1] for chip in range(CHIPS)]

    packed = pl.pallas_call(
        pack_kernel,
        out_shape=jax.ShapeDtypeStruct((CHIPS * SLOT, HEAD), jnp.bfloat16),
        in_specs=[VMEM],
        out_specs=VMEM,
        compiler_params=pltpu.CompilerParams(vmem_limit_bytes=8 * 2**20),
        name="pack",
    )(state[0])
    mods = pl.pallas_call(
        pick_kernel,
        out_shape=jax.ShapeDtypeStruct((8 * FRAMES, HEAD), jnp.float32),
        in_specs=[SMEM, ANY],
        out_specs=VMEM,
        scratch_shapes=[
            pltpu.VMEM((COLUMNS, modulation.shape[1], HEAD), jnp.float32),
            pltpu.SemaphoreType.DMA,
        ],
        compiler_params=pltpu.CompilerParams(vmem_limit_bytes=8 * 2**20),
        name="pick",
    )(noise_level, table)
    heads = lax.all_to_all(packed, "frame", 0, 0, axis_index_groups=same_core, tiled=True)
    slots = lax.all_gather(heads, "frame", axis=0, tiled=True, axis_index_groups=same_chip)
    done = pl.pallas_call(
        attend_kernel,
        out_shape=jax.ShapeDtypeStruct((CHIPS * ROWS, HEAD), jnp.bfloat16),
        in_specs=[SMEM, SMEM, VMEM, VMEM],
        out_specs=VMEM,
        scratch_shapes=[
            pltpu.VMEM((2, 8 * CHIPS, ROWS // 8 * HEAD), jnp.float32),
            pltpu.VMEM((2, FRAMES * HALF, HEAD), jnp.float32),
            pltpu.VMEM((FRAMES * 2 * HALF, HEAD), jnp.bfloat16),
            pltpu.VMEM((FRAMES, HEAD + 16, 2 * HALF), jnp.bfloat16),
            pltpu.VMEM((FRAMES // 2, HEAD, 2 * HALF), jnp.bfloat16),
            pltpu.VMEM((20, 2 * HALF, 2 * HALF), jnp.float32),
        ],
        compiler_params=pltpu.CompilerParams(vmem_limit_bytes=24 * 2**20),
        name="attend",
    )(offset, frame_mask, mods, slots)
    back = lax.all_to_all(done, "frame", 0, 0, axis_index_groups=same_core, tiled=True)
    rows = back.reshape(CHIPS, ROWS, HEAD)[CHIPS - HEADS :][::-1]
    rows = jnp.transpose(rows, (1, 0, 2)).reshape(ROWS, WIDTH)
    passed = lax.ppermute(
        rows, "segment", [(i, (i + 1) % segments) for i in range(segments)]
    )
    return passed[None]


def solution(mesh):
    return jax.shard_map(
        body,
        mesh=mesh,
        in_specs=(P("segment", "frame", None), P("segment", None, None, None), P(), P(), P()),
        out_specs=P("segment", "frame", None),
        check_vma=False,
    )
```

```python
import math

import jax
import jax.numpy as jnp
from jax import lax
from jax.experimental import pallas as pl
from jax.experimental.pallas import tpu as pltpu
from jax.sharding import PartitionSpec as P

HEAD = 128
HEADS = 24
WIDTH = HEAD * HEADS
FRAMES = 8
ROWS = 32
SLOT = ROWS + 8
CHIPS = 32
PER_FRAME = CHIPS // FRAMES
HALF = PER_FRAME * ROWS
COLUMNS = 7

epsilon = 1e-06
negative = -1e30

VMEM = pl.BlockSpec(memory_space=pltpu.VMEM)
SMEM = pl.BlockSpec(memory_space=pltpu.SMEM)
ANY = pl.BlockSpec(memory_space=pl.ANY)


def pack_kernel(state, packed):
    wide = state[...].astype(jnp.float32)
    factor = lax.rsqrt(jnp.sum(wide * wide, axis=-1, keepdims=True) * (1.0 / WIDTH) + epsilon)
    high = factor.astype(jnp.bfloat16).astype(jnp.float32)
    middle = (factor - high).astype(jnp.bfloat16).astype(jnp.float32)
    low = factor - high - middle
    lane = lax.broadcasted_iota(jnp.int32, (8, HEAD), 1)
    factors = jnp.zeros((8, HEAD), jnp.float32)
    for group in range(ROWS // 8):
        for at, piece in enumerate((high, middle, low)):
            rows = jnp.broadcast_to(piece[8 * group : 8 * group + 8], (8, HEAD))
            factors = jnp.where(lane == 32 * group + at, rows, factors)
    for two in range(CHIPS // 2):
        pieces = []
        for slot in (2 * two, 2 * two + 1):
            head = min(CHIPS - 1 - slot, HEADS - 1)
            pieces += [wide[:, HEAD * head : HEAD * (head + 1)], factors]
        both = jnp.concatenate(pieces, axis=0)
        packed[2 * SLOT * two : 2 * SLOT * (two + 1), :] = both.astype(jnp.bfloat16)


def pick_kernel(levels, table, mods, column, sem):
    head = jnp.minimum(lax.axis_index("frame") // 2, HEADS - 1)
    copy = pltpu.make_async_copy(
        table.at[:, :, pl.ds(pl.multiple_of(head * HEAD, HEAD), HEAD)], column, sem
    )
    copy.start()
    copy.wait()
    for frame in range(FRAMES):
        level = levels[frame]
        for c in range(COLUMNS):
            mods[8 * frame + c : 8 * frame + c + 1, :] = column[c, pl.ds(level, 1), :]


def attend_kernel(
    offset, mask, mods, slots, out, factors, normed, keys, values, queries, scores
):
    core = lax.rem(lax.axis_index("frame"), 2)
    last = lax.axis_index("segment") == lax.axis_size("segment") - 1
    shift = jnp.where(last, offset[0], 0)
    chunk = PER_FRAME * SLOT

    def rows_of(frame, c):
        return mods[8 * frame + c : 8 * frame + c + 1, :]

    quarter = lax.broadcasted_iota(jnp.int32, (HEAD, HEAD), 0) >> 5
    spread = jnp.concatenate(
        [jnp.where(quarter == group, 1.0, 0.0) for group in range(ROWS // 8)], axis=1
    ).astype(jnp.bfloat16)
    for part in range(2):
        pieces = []
        for frame in range(FRAMES):
            at = CHIPS * SLOT * part + chunk * (FRAMES - 1 - frame)
            wide = slots[at : at + chunk, :].astype(jnp.float32)
            for slot in range(PER_FRAME):
                pieces.append(wide[SLOT * slot + ROWS : SLOT * (slot + 1)])
        pieces = jnp.concatenate(pieces, axis=0).astype(jnp.bfloat16)
        factors[part] = jnp.dot(pieces, spread, preferred_element_type=jnp.float32)

    def state_of(wide):
        return jnp.concatenate(
            [wide[SLOT * slot : SLOT * slot + ROWS] for slot in range(PER_FRAME)], axis=0
        )

    def prepare(frame):
        for part in range(2):
            at = CHIPS * SLOT * part + chunk * (FRAMES - 1 - frame)
            state = state_of(slots[at : at + chunk, :].astype(jnp.float32))
            factor = jnp.concatenate(
                [
                    factors[
                        part,
                        8 * (PER_FRAME * frame + slot) : 8 * (PER_FRAME * frame + slot + 1),
                        HEAD * group : HEAD * (group + 1),
                    ]
                    for slot in range(PER_FRAME)
                    for group in range(ROWS // 8)
                ],
                axis=0,
            )
            even = (state * factor).astype(jnp.bfloat16).astype(jnp.float32)
            normed[part, HALF * frame : HALF * (frame + 1), :] = even
            key = even * (1.0 + rows_of(frame, 2)) + rows_of(frame, 3)
            value = even * (1.0 + rows_of(frame, 4)) + rows_of(frame, 5)
            row = 2 * HALF * frame + HALF * part
            keys[row : row + HALF, :] = key.astype(jnp.bfloat16)
            values[frame, :HEAD, HALF * part : HALF * (part + 1)] = value.astype(jnp.bfloat16).T
        values[frame, HEAD:, :] = jnp.ones((16, 2 * HALF), jnp.bfloat16)
        even = normed[core, HALF * frame : HALF * (frame + 1), :]
        query = even * (1.0 + rows_of(frame, 0)) + rows_of(frame, 1)
        half = HALF * (frame % 2)
        queries[frame // 2, :, half : half + HALF] = query.astype(jnp.bfloat16).T

    side = lax.broadcasted_iota(jnp.int32, (1, 2 * HALF), 1) < HALF
    rate = math.log2(math.e) / math.sqrt(HEAD)
    wide = 2 * HALF
    scored, weighed = {}, {}

    def score(two, frame):
        barred = jnp.where(
            side,
            jnp.where(mask[2 * two, frame] == 1, 0.0, negative),
            jnp.where(mask[2 * two + 1, frame] == 1, 0.0, negative),
        )
        got = jnp.dot(
            keys[wide * frame : wide * (frame + 1), :],
            queries[two],
            preferred_element_type=jnp.float32,
        )
        scores[two * (two + 1) + frame] = got
        high = jnp.max(got.reshape(wide // 8, 8, wide), axis=0) + barred
        top, bars = scored.get(two, (None, []))
        scored[two] = (high if top is None else jnp.maximum(top, high), [*bars, barred])

    def weigh(two, frame):
        top, bars = scored[two]
        if frame == 0:
            top = jnp.max(top, axis=0, keepdims=True)
            scored[two] = (top, bars)
        less = top - bars[frame]
        weights = jnp.exp2((scores[two * (two + 1) + frame] - less) * rate)
        part = jnp.dot(
            values[frame], weights.astype(jnp.bfloat16), preferred_element_type=jnp.float32
        )
        weighed[two] = part if frame == 0 else weighed[two] + part

    def finish(two):
        total = weighed.pop(two)
        attention = total[:HEAD] * (1.0 / total[HEAD : HEAD + 1])
        attention = attention.astype(jnp.bfloat16).astype(jnp.float32).T
        for side_of, frame in enumerate((2 * two, 2 * two + 1)):
            at = pl.multiple_of(CHIPS * SLOT * core + chunk * (FRAMES - 1 - frame), 16)
            state = state_of(slots[pl.ds(at, chunk), :].astype(jnp.float32))
            rows = attention[HALF * side_of : HALF * (side_of + 1)]
            to = FRAMES - 1 - lax.rem(frame + FRAMES - shift, FRAMES)
            to = pl.multiple_of(HALF * to, HALF)
            out[pl.ds(to, HALF), :] = (state + rows_of(frame, 6) * rows).astype(jnp.bfloat16)

    for frame in range(FRAMES):
        prepare(frame)
        if frame >= 2:
            two = frame // 2 - 1
            for other in range(two + 1):
                score(two, other + (frame % 2) * (two + 1))
    last_pair = FRAMES // 2 - 1
    steps = [(score, last_pair, other) for other in range(FRAMES)]
    for two in reversed(range(last_pair)):
        for frame in range(2 * two + 2):
            if steps:
                step, pair, other = steps.pop(0)
                step(pair, other)
            weigh(two, frame)
        finish(two)
    for frame in range(FRAMES):
        weigh(last_pair, frame)
    finish(last_pair)


def unpack_kernel(heads, rows):
    for head in range(HEADS):
        at = ROWS * (HEADS - 1 - head)
        rows[:, HEAD * head : HEAD * (head + 1)] = heads[at : at + ROWS, :]


def body(state, modulation, noise_level, frame_mask, offset):
    segments = lax.axis_size("segment")
    table = jnp.transpose(modulation[0], (1, 0, 2))
    same_core = [[2 * chip + core for chip in reversed(range(CHIPS))] for core in range(2)]
    same_chip = [[2 * chip, 2 * chip + 1] for chip in range(CHIPS)]

    packed = pl.pallas_call(
        pack_kernel,
        out_shape=jax.ShapeDtypeStruct((CHIPS * SLOT, HEAD), jnp.bfloat16),
        in_specs=[VMEM],
        out_specs=VMEM,
        compiler_params=pltpu.CompilerParams(vmem_limit_bytes=8 * 2**20),
        name="pack",
    )(state[0])
    mods = pl.pallas_call(
        pick_kernel,
        out_shape=jax.ShapeDtypeStruct((8 * FRAMES, HEAD), jnp.float32),
        in_specs=[SMEM, ANY],
        out_specs=VMEM,
        scratch_shapes=[
            pltpu.VMEM((COLUMNS, modulation.shape[1], HEAD), jnp.float32),
            pltpu.SemaphoreType.DMA,
        ],
        compiler_params=pltpu.CompilerParams(vmem_limit_bytes=8 * 2**20),
        name="pick",
    )(noise_level, table)
    heads = lax.all_to_all(packed, "frame", 0, 0, axis_index_groups=same_core, tiled=True)
    slots = lax.all_gather(heads, "frame", axis=0, tiled=True, axis_index_groups=same_chip)
    done = pl.pallas_call(
        attend_kernel,
        out_shape=jax.ShapeDtypeStruct((CHIPS * ROWS, HEAD), jnp.bfloat16),
        in_specs=[SMEM, SMEM, VMEM, VMEM],
        out_specs=VMEM,
        scratch_shapes=[
            pltpu.VMEM((2, 8 * CHIPS, ROWS // 8 * HEAD), jnp.float32),
            pltpu.VMEM((2, FRAMES * HALF, HEAD), jnp.float32),
            pltpu.VMEM((FRAMES * 2 * HALF, HEAD), jnp.bfloat16),
            pltpu.VMEM((FRAMES, HEAD + 16, 2 * HALF), jnp.bfloat16),
            pltpu.VMEM((FRAMES // 2, HEAD, 2 * HALF), jnp.bfloat16),
            pltpu.VMEM((20, 2 * HALF, 2 * HALF), jnp.float32),
        ],
        compiler_params=pltpu.CompilerParams(vmem_limit_bytes=24 * 2**20),
        name="attend",
    )(offset, frame_mask, mods, slots)
    back = lax.all_to_all(done, "frame", 0, 0, axis_index_groups=same_core, tiled=True)
    passed = lax.ppermute(
        back[(CHIPS - HEADS) * ROWS :],
        "segment",
        [(i, (i + 1) % segments) for i in range(segments)],
    )
    rows = pl.pallas_call(
        unpack_kernel,
        out_shape=jax.ShapeDtypeStruct((ROWS, WIDTH), jnp.bfloat16),
        in_specs=[VMEM],
        out_specs=VMEM,
        compiler_params=pltpu.CompilerParams(vmem_limit_bytes=8 * 2**20),
        name="unpack",
    )(passed)
    return rows[None]


def solution(mesh):
    return jax.shard_map(
        body,
        mesh=mesh,
        in_specs=(P("segment", "frame", None), P("segment", None, None, None), P(), P(), P()),
        out_specs=P("segment", "frame", None),
        check_vma=False,
    )
```
